32 devices in a mesh: chan: 16 (over z, y, x), win: 2 (over core).
Axes of the slice: x: 2, y: 2, z: 4, core: 2. Of those that a mesh axis runs over, the one named last changes fastest.
Arguments:
- samples: bfloat16 [2, 2048, 1024], P('win', 'chan'), may hold values from -12 to 12
- pair_tiles: int32 [128, 3], replicated, may hold values from -1 to 15, as said below
Outputs:
- stacks: float32 [128, 64, 128, 128], P('chan', 'win')
The draws below stay inside these ranges and needn't reach their ends.
Inputs may be any that keep to these rules, and one draw needn't show every extreme that they name: Each row of pair_tiles is (a, b, o) with a <= b <= a + 2 and b < 16 and b - 2 <= o <= a + 2, or (-1, -1, -1) for an empty slot. Rows k * 8 to (k + 1) * 8 - 1 hold the tiles of owner k, live rows first. Every pair of blocks with a <= b <= a + 2 is listed exactly once, and some owner has 8 tiles.
All inputs are finite; a program needn't handle non-finite values.
Results may differ from the reference program's by a relative error of at most 0.007.
Values may be sent and summed in bfloat16 or wider, within the bound.
No kernel may reach another device: no remote copies, remote signals or barrier semaphores. Data moves between devices by JAX's collectives and lax.ppermute only.
A program may use at most 64 MiB of HBM per device.

```python
import math
import jax
import jax.numpy as jnp
from jax import lax

CH = 128
NSAMP = 1024
FREQS = 512
LAGS = 128
TILE_CAP = 8
NBLK = 16
CHANNELS = 2048
WINDOWS = 2
STRIDE = 2


def draw_samples(key, part):
    key = jax.random.fold_in(key, 7)
    key_noise, key_gain, key_sinusoid, key_amp, key_phase = jax.random.split(key, 5)
    full_shape = (WINDOWS, CHANNELS, NSAMP)
    gains = jnp.exp(jax.random.uniform(key_gain, (1, CHANNELS, 1), jnp.float32, math.log(0.3), math.log(3.0)))
    noise = jax.random.normal(key_noise, full_shape, jnp.float32)
    amplitude = jax.random.uniform(key_amp, (WINDOWS, CHANNELS, 1), jnp.float32, 0.3, 1.2)
    tone_bin = jax.random.randint(key_sinusoid, (1, CHANNELS, 1), 1, NSAMP // 2)
    sample_index = jnp.arange(NSAMP, dtype=jnp.int32)[None, None, :]
    phase_steps = tone_bin * sample_index % NSAMP
    phases = jax.random.uniform(key_phase, (WINDOWS, CHANNELS, 1), jnp.float32, -math.pi, math.pi)
    phase_angles = 2.0 * math.pi / NSAMP * phase_steps.astype(jnp.float32) + phases
    return jnp.clip(gains * (noise + amplitude * jnp.cos(phase_angles)), -12.0, 12.0).astype(jnp.bfloat16)


def draw_pair_tiles(key, part):
    key = jax.random.fold_in(key, 5)
    key_hot, key_rank, key_side = jax.random.split(key, 3)
    tile_count = 3 * NBLK
    tile_number = jnp.arange(tile_count, dtype=jnp.int32)
    source = tile_number // 3
    target = source + tile_number % 3
    is_live = target < NBLK
    hot_owner = jax.random.randint(key_hot, (), 2, NBLK - 2)
    lowest = jnp.maximum(target - 2, 0)
    highest = jnp.minimum(source + 2, NBLK - 1)
    eligible = is_live & (lowest <= hot_owner) & (hot_owner <= highest)
    scores = jax.random.randint(key_rank, (tile_count,), 0, 65536) * tile_count + tile_number
    scores = jnp.where(eligible, scores, -1)
    ordering = jnp.argsort(-scores, stable=True)
    position = jnp.zeros((tile_count,), jnp.int32).at[ordering].set(tile_number)
    forced = eligible & (position < TILE_CAP)
    side_bit = jax.random.randint(key_side, (tile_count,), 0, 2)
    chosen = jnp.where(side_bit == 0, source, target)
    fallback = jnp.where(side_bit == 0, target, source)
    chosen = jnp.where(chosen == hot_owner, fallback, chosen)
    chosen = jnp.where(chosen == hot_owner, hot_owner + 1, chosen)
    owner_id = jnp.where(forced, hot_owner, chosen)
    owner_id = jnp.where(is_live, owner_id, -1)
    onehot = (owner_id[:, None] == jnp.arange(NBLK, dtype=jnp.int32)[None, :]).astype(jnp.int32)
    slot_rank = jnp.cumsum(onehot, axis=0) - onehot
    slot_number = jnp.sum(slot_rank * onehot, axis=1)
    output_target = jnp.where(is_live, owner_id * TILE_CAP + slot_number, NBLK * TILE_CAP)
    row_values = jnp.stack([source, target, owner_id], axis=1)
    listing = jnp.full((NBLK * TILE_CAP, 3), -1, jnp.int32)
    return listing.at[output_target].set(row_values, mode='drop')


def setup_inputs(seed: int = 0) -> dict:
    keys = jax.random.split(jax.random.key(seed), 3)
    samples = draw_samples(jax.random.fold_in(keys[2], 71), 0)
    pair_tiles = draw_pair_tiles(jax.random.fold_in(keys[2], 71), 0)
    return dict(samples=samples, pair_tiles=pair_tiles)


def forward_table():
    sample_index = jnp.arange(NSAMP, dtype=jnp.int32)
    bin_index = jnp.arange(FREQS, dtype=jnp.int32)
    phase_steps = sample_index[:, None] * bin_index[None, :] % NSAMP
    phase_angles = 2.0 * math.pi / NSAMP * phase_steps.astype(jnp.float32)
    return jnp.concatenate([jnp.cos(phase_angles), -jnp.sin(phase_angles)], axis=1).astype(jnp.bfloat16)

def inverse_dft_matrix():
    bin_index = jnp.arange(FREQS, dtype=jnp.int32)
    lag_values = (jnp.arange(LAGS, dtype=jnp.int32) - LAGS // 2) % NSAMP
    phase_steps = bin_index[:, None] * lag_values[None, :] % NSAMP
    phase_angles = 2.0 * math.pi / NSAMP * phase_steps.astype(jnp.float32)
    return jnp.concatenate([jnp.cos(phase_angles), -jnp.sin(phase_angles)], axis=0).astype(jnp.bfloat16)

def whiten(samples):
    segment_count, channel_count, sample_count = samples.shape
    spectra = jnp.dot(samples.reshape(segment_count * channel_count, sample_count), forward_table(), preferred_element_type=jnp.float32)
    real_part = spectra[:, :FREQS]
    imag_part = spectra[:, FREQS:]
    power_bins = real_part * real_part + imag_part * imag_part
    mean_power = lax.optimization_barrier(jnp.mean(power_bins, axis=1, keepdims=True))
    factor = lax.rsqrt(power_bins + 0.5 * mean_power + 1e-06)
    whitened = (spectra * jnp.concatenate([factor, factor], axis=1)).astype(jnp.bfloat16)
    return whitened.reshape(segment_count, channel_count, 2 * FREQS)

def cross_windows(source_rows, target_rows):
    source_real = source_rows[..., :FREQS]
    source_imag = source_rows[..., FREQS:]
    target_real = target_rows[..., :FREQS]
    target_imag = target_rows[..., FREQS:]
    real_sum = jnp.einsum('wsf,wtf->stf', source_real, target_real) + jnp.einsum('wsf,wtf->stf', source_imag, target_imag)
    imag_sum = jnp.einsum('wsf,wtf->stf', source_imag, target_real) - jnp.einsum('wsf,wtf->stf', source_real, target_imag)
    rounded = jnp.concatenate([real_sum, imag_sum], axis=-1).astype(jnp.bfloat16)
    rounded = lax.optimization_barrier(rounded)
    return rounded.astype(jnp.float32)

def reference(samples, pair_tiles):
    segment_count = samples.shape[0]
    whitened = whiten(samples)
    blocks = whitened.reshape(segment_count, NBLK, CH, 2 * FREQS)
    inverse = inverse_dft_matrix().astype(jnp.float32)
    norm_scale = 1.0 / math.sqrt(FREQS * segment_count)

    def one_tile(tile_number):
        source = tile_number // 3
        target = jnp.minimum(source + tile_number % 3, NBLK - 1)
        source_rows = lax.dynamic_index_in_dim(blocks, source, 1, keepdims=False)[:, ::STRIDE]
        target_rows = lax.dynamic_index_in_dim(blocks, target, 1, keepdims=False)
        cross_spectrum = cross_windows(source_rows.astype(jnp.float32), target_rows.astype(jnp.float32))
        tile_stack = jnp.einsum('stk,kl->slt', cross_spectrum, inverse, precision=lax.Precision.HIGHEST)
        return tile_stack * norm_scale
    all_tiles = lax.map(one_tile, jnp.arange(3 * NBLK, dtype=jnp.int32))
    source_col = pair_tiles[:, 0]
    target_col = pair_tiles[:, 1]
    is_live = pair_tiles[:, 2] >= 0
    lookup = jnp.clip(source_col * 3 + (target_col - source_col), 0, 3 * NBLK - 1).astype(jnp.int32)
    selected = jnp.take(all_tiles, lookup, axis=0)
    return selected * is_live.astype(selected.dtype)[:, None, None, None]
```

```python
import functools
import math

import jax
import jax.numpy as jnp
import numpy as np
from jax import lax
from jax.experimental import pallas as pl
from jax.experimental.pallas import tpu as pltpu
from jax.sharding import PartitionSpec as P

NSAMP = 1024
FREQS = 512
VIRTUAL_SOURCES = 64
LAGS = 128
TILE_CAP = 8
CH = 128
LANES = 128
RE_CHUNKS = FREQS // LANES
CHUNKS = 2 * RE_CHUNKS
NEARBY = 5
VMEM_BYTES = 24 * 1024 * 1024


def forward_table():
    steps = np.arange(NSAMP)[:, None] * np.arange(FREQS)[None, :] % NSAMP
    angles = 2.0 * np.pi / NSAMP * steps
    real = np.cos(angles).reshape(NSAMP, RE_CHUNKS, LANES)
    imag = -np.sin(angles).reshape(NSAMP, RE_CHUNKS, LANES)
    table = np.concatenate([real, imag], axis=2).transpose(1, 0, 2)
    return jnp.asarray(table.astype(np.float32).astype(jnp.bfloat16))


def inverse_table(scale):
    lags = (np.arange(LAGS) - LAGS // 2) % NSAMP
    steps = np.arange(FREQS)[None, :] * lags[:, None] % NSAMP
    angles = 2.0 * np.pi / NSAMP * steps
    table = np.concatenate([np.cos(angles), -np.sin(angles)], axis=1) * scale
    table = table.reshape(LAGS, CHUNKS, LANES).transpose(1, 0, 2)
    return jnp.asarray(table.astype(np.float32).astype(jnp.bfloat16))


def whiten_kernel(samples_hbm, table_hbm, out_ref, samples, table, spectra, sems):
    copies = [pltpu.make_async_copy(samples_hbm, samples, sems.at[RE_CHUNKS])]
    for c in range(RE_CHUNKS):
        copies.append(pltpu.make_async_copy(table_hbm.at[c], table.at[c], sems.at[c]))
    for copy in copies:
        copy.start()
    copies[0].wait()
    rows = samples[0]
    total = jnp.zeros((CH, LANES), jnp.float32)
    for c in range(RE_CHUNKS):
        copies[1 + c].wait()
        part = jnp.dot(rows, table[c], preferred_element_type=jnp.float32)
        spectra[c] = part
        real, imag = part[:, :LANES], part[:, LANES:]
        total = total + (real * real + imag * imag)
    level = jnp.sum(total, axis=1, keepdims=True) * (0.5 / FREQS) + 1e-06
    for c in range(RE_CHUNKS):
        real, imag = spectra[c, :, :LANES], spectra[c, :, LANES:]
        factor = lax.rsqrt(real * real + imag * imag + level)
        out_ref[c] = (real * factor).astype(jnp.bfloat16)
        out_ref[RE_CHUNKS + c] = (imag * factor).astype(jnp.bfloat16)


def whiten(samples):
    return pl.pallas_call(
        whiten_kernel,
        out_shape=jax.ShapeDtypeStruct((CHUNKS, CH, LANES), jnp.bfloat16),
        in_specs=[pl.BlockSpec(memory_space=pltpu.HBM)] * 2,
        out_specs=pl.BlockSpec(memory_space=pltpu.VMEM),
        scratch_shapes=[
            pltpu.VMEM((1, CH, NSAMP), jnp.bfloat16),
            pltpu.VMEM((RE_CHUNKS, NSAMP, 2 * LANES), jnp.bfloat16),
            pltpu.VMEM((RE_CHUNKS, CH, 2 * LANES), jnp.float32),
            pltpu.SemaphoreType.DMA((RE_CHUNKS + 1,)),
        ],
        compiler_params=pltpu.CompilerParams(vmem_limit_bytes=VMEM_BYTES),
        name="whiten",
    )(samples, forward_table())


def cross_chunk(source, target, windows, chunk, s):
    real = imag = None
    for w in range(windows):
        a_re = jnp.broadcast_to(source[w, chunk, pl.ds(s, 1), :], (CH, LANES))
        a_im = jnp.broadcast_to(source[w, RE_CHUNKS + chunk, pl.ds(s, 1), :], (CH, LANES))
        a_re, a_im = a_re.astype(jnp.bfloat16), a_im.astype(jnp.bfloat16)
        b_re, b_im = target[w, chunk], target[w, RE_CHUNKS + chunk]
        re = a_re * b_re + a_im * b_im
        im = a_im * b_re - a_re * b_im
        real = re if real is None else real + re
        imag = im if imag is None else imag + im
    return real, imag


def tile_kernel(config, pairs, table, *refs):
    phase, places, windows, sources, out_scale, first, clears = config
    count = len(places) * windows
    blocks = refs[:count]
    rest = refs[count:] if first else refs[count + 1:]
    out, order, target, source, tiles, zeros, out_sems, zero_sems = rest
    device = lax.axis_index("chan")
    member = lax.axis_index("win")
    base = device * TILE_CAP

    def place_of(block):
        apart = jnp.abs(block - device)
        far = jnp.where(apart == 1, 3, 4)
        near = jnp.where(block == (device ^ 1), 1, jnp.where(block == (device ^ 2), 2, far))
        return jnp.where(apart == 0, 0, near)

    def listed(j, found):
        a, b = pairs[0, base + j], pairs[1, base + j]
        live = pairs[2, base + j] >= 0
        mine = jnp.logical_and(live, jnp.maximum(place_of(a), place_of(b)) == phase)

        @pl.when(mine)
        def _():
            order[found] = j

        return found + mine.astype(jnp.int32)

    found = lax.fori_loop(0, TILE_CAP, listed, 0)

    def clear(j):
        return pltpu.make_async_copy(zeros, out.at[j], zero_sems.at[j])

    def each_empty(act):
        @pl.loop(0, TILE_CAP)
        def _(j):
            @pl.when(pairs[2, base + j] < 0)
            def _():
                act(j)

    if clears:
        zeros[...] = jnp.zeros_like(zeros)
        each_empty(lambda j: clear(j).start())

    def one_tile(i, carry):
        slot = order[i]
        parity = lax.rem(i, 2)
        a_place = place_of(pairs[0, base + slot])
        b_place = place_of(pairs[1, base + slot])
        row = lax.broadcasted_iota(jnp.int32, (sources, CH), 0)
        column = lax.broadcasted_iota(jnp.int32, (sources, CH), 1)
        stride = CH // VIRTUAL_SOURCES
        picks = (column == (member * sources + row) * stride).astype(jnp.float32)
        picks = picks.astype(jnp.bfloat16)
        for j, place in enumerate(places):
            mine = blocks[j * windows : (j + 1) * windows]

            @pl.when(a_place == place)
            def _():
                for w in range(windows):
                    for c in range(CHUNKS):
                        source[w, c] = jnp.dot(
                            picks, mine[w][c], preferred_element_type=jnp.float32
                        )

            @pl.when(b_place == place)
            def _():
                for w in range(windows):
                    target[w] = mine[w][...]

        def leave(j):
            return pltpu.make_async_copy(tiles.at[parity], out.at[j], out_sems.at[parity])

        @pl.when(i >= 2)
        def _():
            leave(slot).wait()

        result = tiles.at[parity]
        group = min(16, sources)

        @pl.loop(0, sources // group)
        def _(g):
            for step in range(group):
                s = g * group + step
                parts = [cross_chunk(source, target, windows, c, s) for c in range(RE_CHUNKS)]
                cross = jnp.concatenate([p[0] for p in parts] + [p[1] for p in parts], axis=1)
                lags = jnp.concatenate([table[c] for c in range(CHUNKS)], axis=1)
                stacked = lax.dot_general(
                    lags, cross, (((1,), (1,)), ((), ())), preferred_element_type=jnp.float32
                )
                result[s] = stacked if out_scale == 1.0 else stacked * out_scale

        leave(slot).start()
        return carry

    lax.fori_loop(0, found, one_tile, 0)

    def drain(i, carry):
        parity = lax.rem(i, 2)
        pltpu.make_async_copy(tiles.at[parity], out.at[order[i]], out_sems.at[parity]).wait()
        return carry

    lax.fori_loop(jnp.maximum(found - 2, 0), found, drain, 0)
    if clears:
        each_empty(lambda j: clear(j).wait())


def tile_call(phase, pairs, table, groups, out, sources, windows, out_scale, clears=False):
    first = out is None
    places = tuple(range(phase + 1))
    config = (phase, places, windows, sources, out_scale, first, clears)
    blocks = [block for group in groups for block in group]
    held = pl.BlockSpec(memory_space=pltpu.VMEM)
    anywhere = pl.BlockSpec(memory_space=pl.ANY)
    operands = [pairs, table, *blocks] + ([] if first else [out])
    specs = [pl.BlockSpec(memory_space=pltpu.SMEM)] + [held] * (1 + len(blocks))
    specs = specs + ([] if first else [anywhere])
    tile_macs = sources * CH * LAGS * 2 * FREQS
    return pl.pallas_call(
        functools.partial(tile_kernel, config),
        out_shape=jax.ShapeDtypeStruct((TILE_CAP, sources, LAGS, CH), jnp.float32),
        in_specs=specs,
        out_specs=anywhere,
        scratch_shapes=[
            pltpu.SMEM((TILE_CAP,), jnp.int32),
            pltpu.VMEM((windows, CHUNKS, CH, LANES), jnp.bfloat16),
            pltpu.VMEM((windows, CHUNKS, sources, LANES), jnp.float32),
            pltpu.VMEM((2, sources, LAGS, CH), jnp.float32),
            pltpu.VMEM((sources if clears else 1, LAGS, CH), jnp.float32),
            pltpu.SemaphoreType.DMA((2,)),
            pltpu.SemaphoreType.DMA((TILE_CAP,)),
        ],
        input_output_aliases={} if first else {len(operands) - 1: 0},
        compiler_params=pltpu.CompilerParams(vmem_limit_bytes=VMEM_BYTES),
        cost_estimate=pl.CostEstimate(
            flops=2 * 2 * tile_macs, bytes_accessed=8 * 1024 * 1024, transcendentals=0
        ),
        name=f"tiles{phase}",
    )(*operands)


def after(out, *blocks):
    arrays = (out, *blocks)
    return pl.pallas_call(
        lambda *refs: None,
        out_shape=[jax.ShapeDtypeStruct(a.shape, a.dtype) for a in arrays],
        in_specs=[pl.BlockSpec(memory_space=pl.ANY)] * len(arrays),
        out_specs=[pl.BlockSpec(memory_space=pl.ANY)] * len(arrays),
        input_output_aliases={i: i for i in range(len(arrays))},
        name="after",
    )(*arrays)


def per_device(samples, pair_tiles):
    devices = lax.axis_size("chan")
    members = lax.axis_size("win")
    windows = samples.shape[0] * members
    sources = VIRTUAL_SOURCES // members
    scale = 1.0 / math.sqrt(FREQS * windows)
    exact = math.frexp(scale)[0] == 0.5
    table = inverse_table(scale if exact else 1.0)
    out_scale = 1.0 if exact else scale
    pairs = pair_tiles.T

    def arriving(block, source_of):
        route = [(source_of(i), i) for i in range(devices) if 0 <= source_of(i) < devices]
        return lax.ppermute(block, "chan", route)

    def all_windows(block):
        if members == 2:
            return [block, lax.ppermute(block, "win", [(0, 1), (1, 0)])]
        gathered = lax.all_gather(block, "win", axis=0)
        return [gathered[w] for w in range(members)]

    call = functools.partial(
        tile_call, pairs=pairs, table=table, sources=sources, windows=windows, out_scale=out_scale
    )
    own = whiten(samples)
    flip_x = arriving(own, lambda i: i ^ 1)
    flip_y = arriving(own, lambda i: i ^ 2)
    next_one = arriving(own, lambda i: i + (-1, 1, -1, 1)[i % 4])
    groups = [all_windows(own)]
    out = call(0, groups=groups, out=None)
    out, flip_x, flip_y, own = after(out, flip_x, flip_y, own)
    groups += [all_windows(flip_x), all_windows(flip_y)]
    next_two = arriving(own, lambda i: i + (-2, -2, 2, 2)[i % 4])
    out = call(1, groups=groups[:2], out=out)
    out, next_one = after(out, next_one)
    groups += [all_windows(next_one)]
    out = call(2, groups=groups[:3], out=out, clears=True)
    out, next_two = after(out, next_two)
    groups += [all_windows(next_two)]
    out = call(3, groups=groups[:4], out=out)
    return call(4, groups=groups, out=out)


def solution(mesh):
    placed = (P("win", "chan", None), P())
    return jax.shard_map(
        per_device,
        mesh=mesh,
        in_specs=placed,
        out_specs=P("chan", "win", None, None),
        check_vma=False,
    )
```

```python
import functools
import math

import jax
import jax.numpy as jnp
from jax import lax
from jax.experimental import pallas as pl
from jax.experimental.pallas import tpu as pltpu
from jax.sharding import PartitionSpec as P

NSAMP = 1024
FREQS = 512
VIRTUAL_SOURCES = 64
LAGS = 128
TILE_CAP = 8
CH = 128
LANES = 128
RE_CHUNKS = FREQS // LANES
CHUNKS = 2 * RE_CHUNKS
FAR = 3
ROWS = 8
QUARTER = NSAMP // 4
VMEM_BYTES = 16 * 1024 * 1024
COSTS = 16, 16, 16
PART = 8


def turns(steps):
    angles = (steps & (NSAMP - 1)).astype(jnp.float32) * (2.0 * math.pi / NSAMP)
    return jnp.cos(angles), jnp.sin(angles)


def turned(rows, slow, fast):
    slow_cos, slow_sin = (part[:, None, :] for part in turns(slow))
    fast_cos, fast_sin = (part[None] for part in turns(fast))
    cos = (slow_cos * fast_cos - slow_sin * fast_sin).reshape(rows, LANES)
    sin = (slow_sin * fast_cos + slow_cos * fast_sin).reshape(rows, LANES)
    return cos, sin


def counts(shape, dimension):
    return lax.broadcasted_iota(jnp.int32, shape, dimension)


def forward_kernel(table):
    blocks = QUARTER // ROWS
    for c in range(RE_CHUNKS):
        slow = counts((blocks, LANES), 0) * ROWS * (counts((blocks, LANES), 1) + c * LANES)
        fast = counts((ROWS, LANES), 0) * (counts((ROWS, LANES), 1) + c * LANES)
        cos, sin = turned(QUARTER, slow, fast)
        table[c, :, :LANES] = cos.astype(jnp.bfloat16)
        table[c, :, LANES:] = (-sin).astype(jnp.bfloat16)


def forward_table():
    return pl.pallas_call(
        forward_kernel,
        out_shape=jax.ShapeDtypeStruct((RE_CHUNKS, QUARTER, 2 * LANES), jnp.bfloat16),
        out_specs=pl.BlockSpec(memory_space=pltpu.VMEM),
        compiler_params=pltpu.CompilerParams(vmem_limit_bytes=VMEM_BYTES),
        name="forward_table",
    )()


def write_inverse(table, scale):
    blocks = LAGS // ROWS
    for c in range(RE_CHUNKS):
        lag = counts((blocks, LANES), 0) * ROWS - LAGS // 2 + NSAMP
        slow = lag * (counts((blocks, LANES), 1) + c * LANES)
        fast = counts((ROWS, LANES), 0) * (counts((ROWS, LANES), 1) + c * LANES)
        cos, sin = turned(LAGS, slow, fast)
        table[c] = (cos * scale).astype(jnp.bfloat16)
        table[RE_CHUNKS + c] = (sin * -scale).astype(jnp.bfloat16)


def coded_slots(pairs, device):
    def place_of(block):
        apart = jnp.abs(block - device)
        far = jnp.where(apart == 1, FAR, FAR + 1)
        near = jnp.where(block == (device ^ 1), 1, jnp.where(block == (device ^ 2), 2, far))
        return jnp.where(apart == 0, 0, near)

    a, b, owner = pairs[0:1, :], pairs[1:2, :], pairs[2:3, :]
    a, b = place_of(a), place_of(b)
    last = jnp.maximum(a, b)
    phase = jnp.where(last == 0, 1, jnp.where(last < FAR, 2, 3))
    slot = counts(owner.shape, 1) - device * TILE_CAP
    code = jnp.where(owner >= 0, phase + 4 * (5 * a + b), 0) << (7 * (slot & 3))
    words = [
        jnp.sum(jnp.where((slot >= 4 * q) & (slot < 4 * q + 4), code, 0)) for q in range(2)
    ]
    return lambda j: (jnp.where(j < 4, words[0], words[1]) >> (7 * (j & 3))) & 127


def whiten_kernel(samples, table, out_ref, spectra):
    rows = [samples[0, :, q * QUARTER : (q + 1) * QUARTER] for q in range(4)]
    bins = counts((QUARTER, LANES), 1)
    sign = (1 - 2 * (bins & 1)).astype(jnp.float32).astype(jnp.bfloat16)
    by_cos = ((1 - (bins & 1)) * (1 - (bins & 2))).astype(jnp.float32).astype(jnp.bfloat16)
    by_sin = ((bins & 1) * (1 - (bins & 2))).astype(jnp.float32).astype(jnp.bfloat16)
    total = jnp.zeros((CH, LANES), jnp.float32)
    for c in range(RE_CHUNKS):
        cos, sin = table[c, :, :LANES], table[c, :, LANES:]
        next_cos = by_cos * cos + by_sin * sin
        next_sin = by_cos * sin - by_sin * cos
        quarters = (cos, sin), (next_cos, next_sin), (sign * cos, sign * sin), (
            sign * next_cos, sign * next_sin,
        )
        part = jnp.zeros((CH, 2 * LANES), jnp.float32)
        for q in range(4):
            part = part + jnp.dot(
                rows[q], jnp.concatenate(quarters[q], axis=1), preferred_element_type=jnp.float32
            )
        spectra[c] = part
        real, imag = part[:, :LANES], part[:, LANES:]
        total = total + (real * real + imag * imag)
    level = jnp.sum(total, axis=1, keepdims=True) * (0.5 / FREQS) + 1e-06
    for c in range(RE_CHUNKS):
        real, imag = spectra[c, :, :LANES], spectra[c, :, LANES:]
        factor = lax.rsqrt(real * real + imag * imag + level)
        out_ref[c] = (real * factor).astype(jnp.bfloat16)
        out_ref[RE_CHUNKS + c] = (imag * factor).astype(jnp.bfloat16)


def whiten(samples):
    return pl.pallas_call(
        whiten_kernel,
        out_shape=jax.ShapeDtypeStruct((CHUNKS, CH, LANES), jnp.bfloat16),
        in_specs=[pl.BlockSpec(memory_space=pltpu.VMEM)] * 2,
        out_specs=pl.BlockSpec(memory_space=pltpu.VMEM),
        scratch_shapes=[pltpu.VMEM((RE_CHUNKS, CH, 2 * LANES), jnp.float32)],
        compiler_params=pltpu.CompilerParams(vmem_limit_bytes=VMEM_BYTES),
        name="whiten",
    )(samples, forward_table())


def cross_chunk(source, target, windows, chunk, s):
    real = imag = None
    for w in range(windows):
        a_re = jnp.broadcast_to(source[w, chunk, pl.ds(s, 1), :], (CH, LANES))
        a_im = jnp.broadcast_to(source[w, RE_CHUNKS + chunk, pl.ds(s, 1), :], (CH, LANES))
        a_re, a_im = a_re.astype(jnp.bfloat16), a_im.astype(jnp.bfloat16)
        b_re, b_im = target[w, chunk], target[w, RE_CHUNKS + chunk]
        re = a_re * b_re + a_im * b_im
        im = a_im * b_re - a_re * b_im
        real = re if real is None else real + re
        imag = im if imag is None else imag + im
    return jnp.concatenate([real, imag], axis=1)


def tile_kernel(config, pairs, *refs):
    phase, windows, sources, scale, first, clears, layout = config
    exact = math.frexp(scale)[0] == 0.5
    count = sum(len(names) for names in layout)
    given = 0 if first else 1
    blocks = refs[given : given + count]
    member = lax.axis_index("win")
    code_of = coded_slots(pairs, lax.axis_index("chan"))
    if first:
        out, table, target, source, rows, tiles, zeros, out_sems, zero_sems = refs[count:]
        write_inverse(table, scale if exact else 1.0)
    else:
        table = refs[0]
        out, target, source, rows, tiles, zeros, out_sems, zero_sems = refs[2 + count :]
    span = sources * CH // VIRTUAL_SOURCES
    parts = [(at, min(PART, sources - at)) for at in range(0, sources, PART)]

    def clear(j):
        return pltpu.make_async_copy(zeros, out.at[j], zero_sems.at[j])

    def each_empty(act):
        @pl.loop(0, TILE_CAP)
        def _(j):
            @pl.when(code_of(j) == 0)
            def _():
                act(j)

    if clears:
        zeros[...] = jnp.zeros_like(zeros)
        each_empty(lambda j: clear(j).start())

    def each_window(place, act):
        position = 0
        for known, kinds in enumerate(layout):
            held = blocks[position : position + len(kinds)]
            position += len(kinds)
            if kinds == ("mine", "other"):

                @pl.when(place == known)
                def _():
                    act(member, held[0])
                    act(1 - member, held[1])

            elif kinds == ("all",):

                @pl.when(place == known)
                def _():
                    for w in range(windows):
                        act(w, held[0].at[w])

            else:

                @pl.when(place == known + member)
                def _():
                    act(member, held[0].at[0])
                    act(1 - member, held[0].at[1])

                @pl.when(place == known + 1 - member)
                def _():
                    act(1 - member, held[1].at[0])
                    act(member, held[1].at[1])

    def leave(parity, j, p):
        at, size = parts[p]
        part = pl.ds(at, size)
        return pltpu.make_async_copy(
            tiles.at[parity, part], out.at[j, part], out_sems.at[parity, p]
        )

    def left(parity):
        for p in range(len(parts)):
            leave(parity, 0, p).wait()

    def take_source(w, ref):
        for c in range(CHUNKS):
            rows[c] = ref[c, pl.ds(pl.multiple_of(member * span, span), span), :].astype(
                jnp.float32
            )
            source[w, c] = rows[c, pl.ds(0, sources, stride=CH // VIRTUAL_SOURCES), :]

    def take_target(w, ref):
        target[w] = ref[...]

    def one_tile(j, place_a, place_b, done):
        parity = done & 1
        each_window(place_a, take_source)
        each_window(place_b, take_target)

        @pl.when(done >= 2)
        def _():
            left(parity)

        for p, (at, size) in enumerate(parts):
            for s in range(at, at + size):
                stacked = jnp.zeros((LAGS, CH), jnp.float32)
                for c in range(RE_CHUNKS):
                    cross = cross_chunk(source, target, windows, c, s)
                    lags = jnp.concatenate([table[c], table[RE_CHUNKS + c]], axis=1)
                    stacked = stacked + lax.dot_general(
                        lags, cross, (((1,), (1,)), ((), ())), preferred_element_type=jnp.float32
                    )
                tiles[parity, s] = stacked if exact else stacked * scale
            leave(parity, j, p).start()

    def one_slot(j, done):
        code = code_of(j)
        mine = (code & 3) == phase + 1
        places = code >> 2
        place_a = lax.div(places, 5)

        @pl.when(mine)
        def _():
            one_tile(j, place_a, places - 5 * place_a, done)

        return done + mine.astype(jnp.int32)

    done = lax.fori_loop(0, TILE_CAP, one_slot, 0)
    for back in (1, 2):

        @pl.when(done >= back)
        def _():
            left((done - back) & 1)

    if clears:
        each_empty(lambda j: clear(j).wait())


def tile_call(phase, known, layout, blocks, out, sources, windows, scale, clears=False):
    first = out is None
    config = (phase, windows, sources, scale, first, clears, layout)
    held = pl.BlockSpec(memory_space=pltpu.VMEM)
    anywhere = pl.BlockSpec(memory_space=pl.ANY)
    operands = [*known, *blocks] + ([] if first else [out])
    specs = [held] * (len(operands) - (not first)) + ([] if first else [anywhere])
    out_shape = [jax.ShapeDtypeStruct((TILE_CAP, sources, LAGS, CH), jnp.float32)]
    out_specs = [anywhere]
    scratch_shapes = [
        pltpu.VMEM((windows, CHUNKS, CH, LANES), jnp.bfloat16),
        pltpu.VMEM((windows, CHUNKS, sources, LANES), jnp.float32),
        pltpu.VMEM((CHUNKS, sources * CH // VIRTUAL_SOURCES, LANES), jnp.float32),
        pltpu.VMEM((2, sources, LAGS, CH), jnp.float32),
        pltpu.VMEM((sources if clears else 1, LAGS, CH), jnp.float32),
        pltpu.SemaphoreType.DMA((2, -(-sources // PART))),
        pltpu.SemaphoreType.DMA((TILE_CAP,)),
    ]
    if first:
        out_shape.append(jax.ShapeDtypeStruct((CHUNKS, LAGS, LANES), jnp.bfloat16))
        out_specs = out_specs + [held]
    results = pl.pallas_call(
        functools.partial(tile_kernel, config),
        out_shape=out_shape,
        in_specs=specs,
        out_specs=out_specs,
        scratch_shapes=scratch_shapes,
        input_output_aliases={} if first else {len(operands) - 1: 0},
        compiler_params=pltpu.CompilerParams(vmem_limit_bytes=VMEM_BYTES),
        cost_estimate=pl.CostEstimate(
            flops=COSTS[phase] * sources * CH * LAGS * 2 * FREQS,
            bytes_accessed=1024 * 1024,
            transcendentals=0,
        ),
        name="tiles{}".format(phase),
    )(*operands)
    return results if first else results[0]


def after_kernel(count, *refs):
    for i in range(count):
        refs[count + 2 + i][...] = refs[1 + i][...]


def after(out, *blocks):
    held = pl.BlockSpec(memory_space=pltpu.VMEM)
    anywhere = pl.BlockSpec(memory_space=pl.ANY)
    arrays = (out, *blocks)
    return pl.pallas_call(
        functools.partial(after_kernel, len(blocks)),
        out_shape=[jax.ShapeDtypeStruct(a.shape, a.dtype) for a in arrays],
        in_specs=[anywhere] + [held] * len(blocks),
        out_specs=[anywhere] + [held] * len(blocks),
        input_output_aliases={0: 0},
        compiler_params=pltpu.CompilerParams(vmem_limit_bytes=VMEM_BYTES),
        name="after",
    )(*arrays)


def sent_on_kernel(x_mine, x_other, y_mine, y_other, out):
    outer = (lax.axis_index("chan") + 1) % 4 < 2
    sends_y = (lax.axis_index("win") == 1) | outer

    @pl.when(sends_y)
    def _():
        out[0], out[1] = y_mine[...], y_other[...]

    @pl.when(jnp.logical_not(sends_y))
    def _():
        out[0], out[1] = x_mine[...], x_other[...]


def sent_on(*near):
    return pl.pallas_call(
        sent_on_kernel,
        out_shape=jax.ShapeDtypeStruct((2, *near[0].shape), near[0].dtype),
        in_specs=[pl.BlockSpec(memory_space=pltpu.VMEM)] * 4,
        out_specs=pl.BlockSpec(memory_space=pltpu.VMEM),
        compiler_params=pltpu.CompilerParams(vmem_limit_bytes=VMEM_BYTES),
        name="sent_on",
    )(*near)


def per_device(samples, pair_tiles):
    devices = lax.axis_size("chan")
    members = lax.axis_size("win")
    windows = samples.shape[0] * members
    sources = VIRTUAL_SOURCES // members
    scale = 1.0 / math.sqrt(FREQS * windows)

    def arriving(block, *routes):
        pairs = []
        for i in range(devices):
            for w in range(members):
                j = i + routes[w % len(routes)][i % 4]
                if 0 <= j < devices:
                    pairs.append((j * members + w, i * members + w))
        return lax.ppermute(block, ("chan", "win"), pairs)

    def swapped(block):
        return lax.ppermute(block, "win", [(0, 1), (1, 0)])

    def gathered(block):
        return lax.all_gather(block, "win", axis=0)

    flip_x, flip_y = (1, -1, 1, -1), (2, 2, -2, -2)
    to_third, to_fourth = (-2, -1, 1, 2), (-4, -4, 4, 4)

    pairs = pair_tiles.T
    own = whiten(samples)
    call = functools.partial(tile_call, sources=sources, windows=windows, scale=scale)
    near = [arriving(own, flip_x), arriving(own, flip_y)]
    if members == 2:
        pair = ("mine", "other")
        blocks = [own, swapped(own)]
        out, table = call(0, [pairs], (pair,), blocks, out=None)
        out, *near = after(out, *near)
        near = [near[0], swapped(near[0]), near[1], swapped(near[1])]
        far = arriving(sent_on(*near), to_third, to_fourth)
        blocks = blocks + near
        out = call(1, [pairs, table], (pair,) * 3, blocks, out=out, clears=True)
        out, far = after(out, far)
        layout = (pair,) * 3 + (("far", "far"),)
        return call(2, [pairs, table], layout, blocks + [far, swapped(far)], out=out)
    layout = (("all",),)
    blocks = [gathered(own)]
    out, table = call(0, [pairs], layout, blocks, out=None)
    outer = (lax.axis_index("chan") + 1) % 4 < 2
    far = [
        arriving(jnp.where(outer, near[1], near[0]), to_third), arriving(near[1], to_fourth)
    ]
    blocks = blocks + [gathered(block) for block in near]
    out = call(1, [pairs, table], layout * 3, blocks, out=out, clears=True)
    blocks = blocks + [gathered(block) for block in far]
    return call(2, [pairs, table], layout * 5, blocks, out=out)


def solution(mesh):
    placed = (P("win", "chan", None), P())
    return jax.shard_map(
        per_device,
        mesh=mesh,
        in_specs=placed,
        out_specs=P("chan", "win", None, None),
        check_vma=False,
    )
```

```python
import functools
import math

import jax
import jax.numpy as jnp
from jax import lax
from jax.experimental import pallas as pl
from jax.experimental.pallas import tpu as pltpu
from jax.sharding import PartitionSpec as P

NSAMP = 1024
FREQS = 512
VIRTUAL_SOURCES = 64
LAGS = 128
TILE_CAP = 8
CH = 128
LANES = 128
RE_CHUNKS = FREQS // LANES
CHUNKS = 2 * RE_CHUNKS
FAR = 3
NEARBY = 5
ROWS = 8
QUARTER = NSAMP // 4
VMEM_BYTES = 16 * 1024 * 1024
COSTS = 1, 16, 16, 16
PART = 8


def turns(steps):
    angles = (steps & (NSAMP - 1)).astype(jnp.float32) * (2.0 * math.pi / NSAMP)
    return jnp.cos(angles), jnp.sin(angles)


def turned(rows, slow, fast):
    slow_cos, slow_sin = (part[:, None, :] for part in turns(slow))
    fast_cos, fast_sin = (part[None] for part in turns(fast))
    cos = (slow_cos * fast_cos - slow_sin * fast_sin).reshape(rows, LANES)
    sin = (slow_sin * fast_cos + slow_cos * fast_sin).reshape(rows, LANES)
    return cos, sin


def counts(shape, dimension):
    return lax.broadcasted_iota(jnp.int32, shape, dimension)


def forward_kernel(table):
    blocks = QUARTER // ROWS
    for c in range(RE_CHUNKS):
        slow = counts((blocks, LANES), 0) * ROWS * (counts((blocks, LANES), 1) + c * LANES)
        fast = counts((ROWS, LANES), 0) * (counts((ROWS, LANES), 1) + c * LANES)
        cos, sin = turned(QUARTER, slow, fast)
        table[c, :, :LANES] = cos.astype(jnp.bfloat16)
        table[c, :, LANES:] = (-sin).astype(jnp.bfloat16)


def forward_table():
    return pl.pallas_call(
        forward_kernel,
        out_shape=jax.ShapeDtypeStruct((RE_CHUNKS, QUARTER, 2 * LANES), jnp.bfloat16),
        out_specs=pl.BlockSpec(memory_space=pltpu.VMEM),
        compiler_params=pltpu.CompilerParams(vmem_limit_bytes=VMEM_BYTES),
        name="forward_table",
    )()


def write_inverse(table, scale):
    blocks = LAGS // ROWS
    for c in range(RE_CHUNKS):
        lag = counts((blocks, LANES), 0) * ROWS - LAGS // 2 + NSAMP
        slow = lag * (counts((blocks, LANES), 1) + c * LANES)
        fast = counts((ROWS, LANES), 0) * (counts((ROWS, LANES), 1) + c * LANES)
        cos, sin = turned(LAGS, slow, fast)
        table[c] = (cos * scale).astype(jnp.bfloat16)
        table[RE_CHUNKS + c] = (sin * -scale).astype(jnp.bfloat16)


def coded_slots(pairs, device, late):
    def place_of(block):
        apart = jnp.abs(block - device)
        far = jnp.where(apart == 1, FAR, FAR + 1)
        near = jnp.where(block == (device ^ 1), 1, jnp.where(block == (device ^ 2), 2, far))
        return jnp.where(apart == 0, 0, near)

    a, b, owner = pairs[0:1, :], pairs[1:2, :], pairs[2:3, :]
    a, b = place_of(a), place_of(b)
    last = jnp.maximum(a, b)
    far = jnp.where((a == late) | (b == late), 4, 3)
    phase = jnp.where(last == 0, 1, jnp.where(last < FAR, 2, far))
    slot = counts(owner.shape, 1) - device * TILE_CAP
    code = jnp.where(owner >= 0, phase + 8 * (5 * a + b), 0) << (8 * (slot & 3))
    words = [
        jnp.sum(jnp.where((slot >= 4 * q) & (slot < 4 * q + 4), code, 0)) for q in range(2)
    ]
    return lambda j: (jnp.where(j < 4, words[0], words[1]) >> (8 * (j & 3))) & 255


def whiten_kernel(samples, table, out_ref, spectra):
    rows = [samples[0, :, q * QUARTER : (q + 1) * QUARTER] for q in range(4)]
    bins = counts((QUARTER, LANES), 1)
    sign = (1 - 2 * (bins & 1)).astype(jnp.float32).astype(jnp.bfloat16)
    by_cos = ((1 - (bins & 1)) * (1 - (bins & 2))).astype(jnp.float32).astype(jnp.bfloat16)
    by_sin = ((bins & 1) * (1 - (bins & 2))).astype(jnp.float32).astype(jnp.bfloat16)
    total = jnp.zeros((CH, LANES), jnp.float32)
    for c in range(RE_CHUNKS):
        cos, sin = table[c, :, :LANES], table[c, :, LANES:]
        next_cos = by_cos * cos + by_sin * sin
        next_sin = by_cos * sin - by_sin * cos
        quarters = (cos, sin), (next_cos, next_sin), (sign * cos, sign * sin), (
            sign * next_cos, sign * next_sin,
        )
        part = jnp.zeros((CH, 2 * LANES), jnp.float32)
        for q in range(4):
            part = part + jnp.dot(
                rows[q], jnp.concatenate(quarters[q], axis=1), preferred_element_type=jnp.float32
            )
        spectra[c] = part
        real, imag = part[:, :LANES], part[:, LANES:]
        total = total + (real * real + imag * imag)
    level = jnp.sum(total, axis=1, keepdims=True) * (0.5 / FREQS) + 1e-06
    for c in range(RE_CHUNKS):
        real, imag = spectra[c, :, :LANES], spectra[c, :, LANES:]
        factor = lax.rsqrt(real * real + imag * imag + level)
        out_ref[c] = (real * factor).astype(jnp.bfloat16)
        out_ref[RE_CHUNKS + c] = (imag * factor).astype(jnp.bfloat16)


def whiten(samples):
    return pl.pallas_call(
        whiten_kernel,
        out_shape=jax.ShapeDtypeStruct((CHUNKS, CH, LANES), jnp.bfloat16),
        in_specs=[pl.BlockSpec(memory_space=pltpu.VMEM)] * 2,
        out_specs=pl.BlockSpec(memory_space=pltpu.VMEM),
        scratch_shapes=[pltpu.VMEM((RE_CHUNKS, CH, 2 * LANES), jnp.float32)],
        compiler_params=pltpu.CompilerParams(vmem_limit_bytes=VMEM_BYTES),
        name="whiten",
    )(samples, forward_table())


def cross_chunk(source, target, windows, chunk, s):
    real = imag = None
    for w in range(windows):
        a_re = jnp.broadcast_to(source[w, chunk, pl.ds(s, 1), :], (CH, LANES))
        a_im = jnp.broadcast_to(source[w, RE_CHUNKS + chunk, pl.ds(s, 1), :], (CH, LANES))
        a_re, a_im = a_re.astype(jnp.bfloat16), a_im.astype(jnp.bfloat16)
        b_re, b_im = target[w, chunk], target[w, RE_CHUNKS + chunk]
        re = a_re * b_re + a_im * b_im
        im = a_im * b_re - a_re * b_im
        real = re if real is None else real + re
        imag = im if imag is None else imag + im
    return jnp.concatenate([real, imag], axis=1)


def tile_kernel(config, pairs, *refs):
    phase, windows, sources, scale, first, clears, layout = config
    exact = math.frexp(scale)[0] == 0.5
    count = sum(held for _, _, held in layout)
    given = 0 if first else 1
    blocks = refs[given : given + count]
    member = lax.axis_index("win")
    late = FAR + 1 - member if lax.axis_size("win") == 2 else NEARBY
    code_of = coded_slots(pairs, lax.axis_index("chan"), late)
    if first:
        out, table, target, source, rows, tiles, zeros, out_sems, zero_sems = refs[count:]
        write_inverse(table, scale if exact else 1.0)
    else:
        table = refs[0]
        out, target, source, rows, tiles, zeros, out_sems, zero_sems = refs[2 + count :]
    span = sources * CH // VIRTUAL_SOURCES
    parts = [(at, min(PART, sources - at)) for at in range(0, sources, PART)]

    def clear(j):
        return pltpu.make_async_copy(zeros, out.at[j], zero_sems.at[j])

    def each_empty(act):
        @pl.loop(0, TILE_CAP)
        def _(j):
            @pl.when(code_of(j) == 0)
            def _():
                act(j)

    if clears:
        zeros[...] = jnp.zeros_like(zeros)
        each_empty(lambda j: clear(j).start())

    def each_window(place, act):
        position = 0
        for known, kind, held in layout:
            held = blocks[position : position + held]
            position += len(held)
            if kind == "all":

                @pl.when(place == known)
                def _():
                    for w in range(windows):
                        act(w, held[0].at[w])

                continue
            for i, ref in enumerate(held):
                nearer = (1 - member) if i else member

                @pl.when(place == (known + nearer if kind == "two" else known))
                def _():
                    act(nearer, ref if kind == "own" else ref.at[0])
                    if kind == "two":
                        act(1 - nearer, ref.at[1])

    def leave(parity, j, p):
        at, size = parts[p]
        part = pl.ds(at, size)
        return pltpu.make_async_copy(
            tiles.at[parity, part], out.at[j, part], out_sems.at[parity, p]
        )

    def left(parity):
        for p in range(len(parts)):
            leave(parity, 0, p).wait()

    def take_source(w, ref):
        for c in range(CHUNKS):
            rows[c] = ref[c, pl.ds(pl.multiple_of(member * span, span), span), :].astype(
                jnp.float32
            )
            source[w, c] = rows[c, pl.ds(0, sources, stride=CH // VIRTUAL_SOURCES), :]

    def take_target(w, ref):
        target[w] = ref[...]

    def one_tile(j, place_a, place_b, done):
        parity = done & 1
        each_window(place_a, take_source)
        each_window(place_b, take_target)

        @pl.when(done >= 2)
        def _():
            left(parity)

        for p, (at, size) in enumerate(parts):
            for s in range(at, at + size):
                stacked = jnp.zeros((LAGS, CH), jnp.float32)
                for c in range(RE_CHUNKS):
                    cross = cross_chunk(source, target, windows, c, s)
                    lags = jnp.concatenate([table[c], table[RE_CHUNKS + c]], axis=1)
                    stacked = stacked + lax.dot_general(
                        lags, cross, (((1,), (1,)), ((), ())), preferred_element_type=jnp.float32
                    )
                tiles[parity, s] = stacked if exact else stacked * scale
            leave(parity, j, p).start()

    def one_slot(j, done):
        code = code_of(j)
        mine = (code & 7) == phase
        places = code >> 3
        place_a = lax.div(places, 5)

        @pl.when(mine)
        def _():
            one_tile(j, place_a, places - 5 * place_a, done)

        return done + mine.astype(jnp.int32)

    done = lax.fori_loop(0, TILE_CAP, one_slot, 0)
    for back in (1, 2):

        @pl.when(done >= back)
        def _():
            left((done - back) & 1)

    if clears:
        each_empty(lambda j: clear(j).wait())


def tile_call(phase, known, layout, blocks, out, sources, windows, scale, clears=False):
    first = out is None
    config = (phase, windows, sources, scale, first, clears, layout)
    held = pl.BlockSpec(memory_space=pltpu.VMEM)
    anywhere = pl.BlockSpec(memory_space=pl.ANY)
    operands = [*known, *blocks] + ([] if first else [out])
    specs = [held] * (len(operands) - (not first)) + ([] if first else [anywhere])
    out_shape = [jax.ShapeDtypeStruct((TILE_CAP, sources, LAGS, CH), jnp.float32)]
    out_specs = [anywhere]
    scratch_shapes = [
        pltpu.VMEM((windows, CHUNKS, CH, LANES), jnp.bfloat16),
        pltpu.VMEM((windows, CHUNKS, sources, LANES), jnp.float32),
        pltpu.VMEM((CHUNKS, sources * CH // VIRTUAL_SOURCES, LANES), jnp.float32),
        pltpu.VMEM((2, sources, LAGS, CH), jnp.float32),
        pltpu.VMEM((sources if clears else 1, LAGS, CH), jnp.float32),
        pltpu.SemaphoreType.DMA((2, -(-sources // PART))),
        pltpu.SemaphoreType.DMA((TILE_CAP,)),
    ]
    if first:
        out_shape.append(jax.ShapeDtypeStruct((CHUNKS, LAGS, LANES), jnp.bfloat16))
        out_specs = out_specs + [held]
    results = pl.pallas_call(
        functools.partial(tile_kernel, config),
        out_shape=out_shape,
        in_specs=specs,
        out_specs=out_specs,
        scratch_shapes=scratch_shapes,
        input_output_aliases={} if first else {len(operands) - 1: 0},
        compiler_params=pltpu.CompilerParams(vmem_limit_bytes=VMEM_BYTES),
        cost_estimate=pl.CostEstimate(
            flops=COSTS[phase - 1] * sources * CH * LAGS * 2 * FREQS,
            bytes_accessed=1024 * 1024,
            transcendentals=0,
        ),
        name="tiles{}".format(phase),
    )(*operands)
    return results if first else results[0]


def after_kernel(count, *refs):
    for i in range(count):
        refs[count + 2 + i][...] = refs[1 + i][...]


def after(out, *blocks):
    held = pl.BlockSpec(memory_space=pltpu.VMEM)
    anywhere = pl.BlockSpec(memory_space=pl.ANY)
    arrays = (out, *blocks)
    return pl.pallas_call(
        functools.partial(after_kernel, len(blocks)),
        out_shape=[jax.ShapeDtypeStruct(a.shape, a.dtype) for a in arrays],
        in_specs=[anywhere] + [held] * len(blocks),
        out_specs=[anywhere] + [held] * len(blocks),
        input_output_aliases={0: 0},
        compiler_params=pltpu.CompilerParams(vmem_limit_bytes=VMEM_BYTES),
        name="after",
    )(*arrays)


def paired_kernel(mine, other, out):
    out[0], out[1] = mine[...], other[...]


def paired(mine, other):
    return pl.pallas_call(
        paired_kernel,
        out_shape=jax.ShapeDtypeStruct((2, *mine.shape), mine.dtype),
        in_specs=[pl.BlockSpec(memory_space=pltpu.VMEM)] * 2,
        out_specs=pl.BlockSpec(memory_space=pltpu.VMEM),
        compiler_params=pltpu.CompilerParams(vmem_limit_bytes=VMEM_BYTES),
        name="paired",
    )(mine, other)


def per_device(samples, pair_tiles):
    devices = lax.axis_size("chan")
    members = lax.axis_size("win")
    windows = samples.shape[0] * members
    sources = VIRTUAL_SOURCES // members
    scale = 1.0 / math.sqrt(FREQS * windows)

    def arriving(block, *routes):
        pairs = []
        for i in range(devices):
            for w in range(members):
                j = i + routes[w % len(routes)][i % 4]
                if 0 <= j < devices:
                    pairs.append((j * members + w, i * members + w))
        return lax.ppermute(block, ("chan", "win"), pairs)

    def swapped(block):
        return lax.ppermute(block, "win", [(0, 1), (1, 0)])

    def gathered(block):
        return lax.all_gather(block, "win", axis=0)

    flip_x, flip_y = (1, -1, 1, -1), (2, 2, -2, -2)
    to_third, to_fourth = (-2, 2, -2, 2), (-4, -4, 4, 4)

    pairs = pair_tiles.T
    own = whiten(samples)
    call = functools.partial(tile_call, sources=sources, windows=windows, scale=scale)
    if members == 2:
        blocks = [own, swapped(own)]
        near = arriving(paired(*blocks), flip_x, flip_y)
        layout = ((0, "own", 2),)
        out, inverse = call(1, [pairs], layout, blocks, out=None)
        known = [pairs, inverse]
        out, near = after(out, near)
        far = arriving(near, to_third, to_fourth)
        blocks = blocks + [near, swapped(near)]
        layout = layout + ((1, "two", 2),)
        out = call(2, known, layout, blocks, out=out, clears=True)
        out, far = after(out, far)
        far = [far, swapped(far)]
        out = call(3, known, layout + ((FAR, "two", 1),), blocks + far[:1], out=out)
        return call(4, known, layout + ((FAR, "two", 2),), blocks + far, out=out)
    layout = tuple((place, "all", 1) for place in range(NEARBY))
    near = [arriving(own, flip_x), arriving(own, flip_y)]
    blocks = [gathered(own)]
    out, inverse = call(1, [pairs], layout[:1], blocks, out=None)
    known = [pairs, inverse]
    far = [arriving(near[0], to_third), arriving(near[1], to_fourth)]
    blocks = blocks + [gathered(block) for block in near]
    out = call(2, known, layout[:FAR], blocks, out=out, clears=True)
    blocks = blocks + [gathered(block) for block in far]
    return call(3, known, layout, blocks, out=out)


def solution(mesh):
    placed = (P("win", "chan", None), P())
    return jax.shard_map(
        per_device,
        mesh=mesh,
        in_specs=placed,
        out_specs=P("chan", "win", None, None),
        check_vma=False,
    )
```

```python
import functools
import math

import jax
import jax.numpy as jnp
from jax import lax
from jax.experimental import pallas as pl
from jax.experimental.pallas import tpu as pltpu
from jax.sharding import PartitionSpec as P

NSAMP = 1024
FREQS = 512
VIRTUAL_SOURCES = 64
LAGS = 128
TILE_CAP = 8
CH = 128
LANES = 128
RE_CHUNKS = FREQS // LANES
CHUNKS = 2 * RE_CHUNKS
FAR = 3
NEARBY = 5
ROWS = 8
QUARTER = NSAMP // 4
VMEM_BYTES = 16 * 1024 * 1024
COSTS = 1, 16, 16, 16
PART = 8


def turns(steps):
    angles = (steps & (NSAMP - 1)).astype(jnp.float32) * (2.0 * math.pi / NSAMP)
    return jnp.cos(angles), jnp.sin(angles)


def turned(rows, slow, fast):
    slow_cos, slow_sin = (part[:, None, :] for part in turns(slow))
    fast_cos, fast_sin = (part[None] for part in turns(fast))
    cos = (slow_cos * fast_cos - slow_sin * fast_sin).reshape(rows, LANES)
    sin = (slow_sin * fast_cos + slow_cos * fast_sin).reshape(rows, LANES)
    return cos, sin


def counts(shape, dimension):
    return lax.broadcasted_iota(jnp.int32, shape, dimension)


def forward_kernel(table):
    blocks = QUARTER // ROWS
    for c in range(RE_CHUNKS):
        slow = counts((blocks, LANES), 0) * ROWS * (counts((blocks, LANES), 1) + c * LANES)
        fast = counts((ROWS, LANES), 0) * (counts((ROWS, LANES), 1) + c * LANES)
        cos, sin = turned(QUARTER, slow, fast)
        table[c, :, :LANES] = cos.astype(jnp.bfloat16)
        table[c, :, LANES:] = (-sin).astype(jnp.bfloat16)


def forward_table():
    return pl.pallas_call(
        forward_kernel,
        out_shape=jax.ShapeDtypeStruct((RE_CHUNKS, QUARTER, 2 * LANES), jnp.bfloat16),
        out_specs=pl.BlockSpec(memory_space=pltpu.VMEM),
        compiler_params=pltpu.CompilerParams(vmem_limit_bytes=VMEM_BYTES),
        name="forward_table",
    )()


def write_inverse(table, scale):
    blocks = LAGS // ROWS
    for c in range(RE_CHUNKS):
        lag = counts((blocks, LANES), 0) * ROWS - LAGS // 2 + NSAMP
        slow = lag * (counts((blocks, LANES), 1) + c * LANES)
        fast = counts((ROWS, LANES), 0) * (counts((ROWS, LANES), 1) + c * LANES)
        cos, sin = turned(LAGS, slow, fast)
        table[c] = (cos * scale).astype(jnp.bfloat16)
        table[RE_CHUNKS + c] = (sin * -scale).astype(jnp.bfloat16)


def coded_slots(pairs, device, late):
    def place_of(block):
        apart = jnp.abs(block - device)
        far = jnp.where(apart == 1, FAR, FAR + 1)
        near = jnp.where(block == (device ^ 1), 1, jnp.where(block == (device ^ 2), 2, far))
        return jnp.where(apart == 0, 0, near)

    a, b, owner = pairs[0:1, :], pairs[1:2, :], pairs[2:3, :]
    a, b = place_of(a), place_of(b)
    last = jnp.maximum(a, b)
    far = jnp.where((a == late) | (b == late), 4, 3)
    phase = jnp.where(last == 0, 1, jnp.where(last < FAR, 2, far))
    slot = counts(owner.shape, 1) - device * TILE_CAP
    code = jnp.where(owner >= 0, phase + 8 * (5 * a + b), 0) << (8 * (slot & 3))
    words = [
        jnp.sum(jnp.where((slot >= 4 * q) & (slot < 4 * q + 4), code, 0)) for q in range(2)
    ]
    return lambda j: (jnp.where(j < 4, words[0], words[1]) >> (8 * (j & 3))) & 255


def whiten_kernel(samples, table, out_ref, spectra):
    rows = [samples[0, :, q * QUARTER : (q + 1) * QUARTER] for q in range(4)]
    bins = counts((QUARTER, LANES), 1)
    sign = (1 - 2 * (bins & 1)).astype(jnp.float32).astype(jnp.bfloat16)
    by_cos = ((1 - (bins & 1)) * (1 - (bins & 2))).astype(jnp.float32).astype(jnp.bfloat16)
    by_sin = ((bins & 1) * (1 - (bins & 2))).astype(jnp.float32).astype(jnp.bfloat16)
    total = jnp.zeros((CH, LANES), jnp.float32)
    for c in range(RE_CHUNKS):
        cos, sin = table[c, :, :LANES], table[c, :, LANES:]
        next_cos = by_cos * cos + by_sin * sin
        next_sin = by_cos * sin - by_sin * cos
        quarters = (cos, sin), (next_cos, next_sin), (sign * cos, sign * sin), (
            sign * next_cos, sign * next_sin,
        )
        part = jnp.zeros((CH, 2 * LANES), jnp.float32)
        for q in range(4):
            part = part + jnp.dot(
                rows[q], jnp.concatenate(quarters[q], axis=1), preferred_element_type=jnp.float32
            )
        spectra[c] = part
        real, imag = part[:, :LANES], part[:, LANES:]
        total = total + (real * real + imag * imag)
    level = jnp.sum(total, axis=1, keepdims=True) * (0.5 / FREQS) + 1e-06
    for c in range(RE_CHUNKS):
        real, imag = spectra[c, :, :LANES], spectra[c, :, LANES:]
        factor = lax.rsqrt(real * real + imag * imag + level)
        out_ref[c] = (real * factor).astype(jnp.bfloat16)
        out_ref[RE_CHUNKS + c] = (imag * factor).astype(jnp.bfloat16)


def whiten(samples):
    return pl.pallas_call(
        whiten_kernel,
        out_shape=jax.ShapeDtypeStruct((CHUNKS, CH, LANES), jnp.bfloat16),
        in_specs=[pl.BlockSpec(memory_space=pltpu.VMEM)] * 2,
        out_specs=pl.BlockSpec(memory_space=pltpu.VMEM),
        scratch_shapes=[pltpu.VMEM((RE_CHUNKS, CH, 2 * LANES), jnp.float32)],
        compiler_params=pltpu.CompilerParams(vmem_limit_bytes=VMEM_BYTES),
        name="whiten",
    )(samples, forward_table())


def cross_chunk(source, target, windows, chunk, s):
    real = imag = None
    for w in range(windows):
        a_re = jnp.broadcast_to(source[w, chunk, pl.ds(s, 1), :], (CH, LANES))
        a_im = jnp.broadcast_to(source[w, RE_CHUNKS + chunk, pl.ds(s, 1), :], (CH, LANES))
        a_re, a_im = a_re.astype(jnp.bfloat16), a_im.astype(jnp.bfloat16)
        b_re, b_im = target[w, chunk], target[w, RE_CHUNKS + chunk]
        re = a_re * b_re + a_im * b_im
        im = a_im * b_re - a_re * b_im
        real = re if real is None else real + re
        imag = im if imag is None else imag + im
    return jnp.concatenate([real, imag], axis=1)


def tile_kernel(config, pairs, *refs):
    phase, windows, sources, scale, first, clears, layout = config
    exact = math.frexp(scale)[0] == 0.5
    count = sum(held for _, _, held in layout)
    given = 0 if first else 1
    blocks = refs[given : given + count]
    member = lax.axis_index("win")
    late = FAR + 1 - member if lax.axis_size("win") == 2 else NEARBY
    code_of = coded_slots(pairs, lax.axis_index("chan"), late)
    if first:
        out, table, target, source, rows, tiles, zeros, out_sems, zero_sems = refs[count:]
        write_inverse(table, scale if exact else 1.0)
    else:
        table = refs[0]
        out, target, source, rows, tiles, zeros, out_sems, zero_sems = refs[2 + count :]
    span = sources * CH // VIRTUAL_SOURCES
    parts = [(at, min(PART, sources - at)) for at in range(0, sources, PART)]

    def clear(j):
        return pltpu.make_async_copy(zeros, out.at[j], zero_sems.at[j])

    def each_empty(act):
        @pl.when(code_of(TILE_CAP - 1) == 0)
        def _():
            @pl.loop(0, TILE_CAP)
            def _(j):
                @pl.when(code_of(j) == 0)
                def _():
                    act(j)

    if clears:

        @pl.when(code_of(TILE_CAP - 1) == 0)
        def _():
            zeros[...] = jnp.zeros_like(zeros)

        each_empty(lambda j: clear(j).start())

    def each_window(place, act):
        position = 0
        for known, kind, held in layout:
            held = blocks[position : position + held]
            position += len(held)
            if kind == "all":

                @pl.when(place == known)
                def _():
                    for w in range(windows):
                        act(w, held[0].at[w])

                continue
            for i, ref in enumerate(held):
                nearer = (1 - member) if i else member

                @pl.when(place == (known + nearer if kind == "two" else known))
                def _():
                    act(nearer, ref if kind == "own" else ref.at[0])
                    if kind == "two":
                        act(1 - nearer, ref.at[1])

    def leave(parity, j, p):
        at, size = parts[p]
        part = pl.ds(at, size)
        return pltpu.make_async_copy(
            tiles.at[parity, part], out.at[j, part], out_sems.at[parity, p]
        )

    def left(parity):
        for p in range(len(parts)):
            leave(parity, 0, p).wait()

    def take_source(w, ref):
        for c in range(CHUNKS):
            rows[c] = ref[c, pl.ds(pl.multiple_of(member * span, span), span), :].astype(
                jnp.float32
            )
            source[w, c] = rows[c, pl.ds(0, sources, stride=CH // VIRTUAL_SOURCES), :]

    def take_target(w, ref):
        target[w] = ref[...]

    def one_tile(j, place_a, place_b, done):
        parity = done & 1
        each_window(place_a, take_source)
        each_window(place_b, take_target)

        @pl.when(done >= 2)
        def _():
            left(parity)

        for p, (at, size) in enumerate(parts):
            for s in range(at, at + size):
                stacked = jnp.zeros((LAGS, CH), jnp.float32)
                for c in range(RE_CHUNKS):
                    cross = cross_chunk(source, target, windows, c, s)
                    lags = jnp.concatenate([table[c], table[RE_CHUNKS + c]], axis=1)
                    stacked = stacked + lax.dot_general(
                        lags, cross, (((1,), (1,)), ((), ())), preferred_element_type=jnp.float32
                    )
                tiles[parity, s] = stacked if exact else stacked * scale
            leave(parity, j, p).start()

    def one_slot(j, done):
        code = code_of(j)
        mine = (code & 7) == phase
        places = code >> 3
        place_a = lax.div(places, 5)

        @pl.when(mine)
        def _():
            one_tile(j, place_a, places - 5 * place_a, done)

        return done + mine.astype(jnp.int32)

    done = lax.fori_loop(0, TILE_CAP, one_slot, 0)
    for back in (1, 2):

        @pl.when(done >= back)
        def _():
            left((done - back) & 1)

    if clears:
        each_empty(lambda j: clear(j).wait())


def tile_call(phase, known, layout, blocks, out, sources, windows, scale, clears=False):
    first = out is None
    config = (phase, windows, sources, scale, first, clears, layout)
    held = pl.BlockSpec(memory_space=pltpu.VMEM)
    anywhere = pl.BlockSpec(memory_space=pl.ANY)
    operands = [*known, *blocks] + ([] if first else [out])
    specs = [held] * (len(operands) - (not first)) + ([] if first else [anywhere])
    out_shape = [jax.ShapeDtypeStruct((TILE_CAP, sources, LAGS, CH), jnp.float32)]
    out_specs = [anywhere]
    scratch_shapes = [
        pltpu.VMEM((windows, CHUNKS, CH, LANES), jnp.bfloat16),
        pltpu.VMEM((windows, CHUNKS, sources, LANES), jnp.float32),
        pltpu.VMEM((CHUNKS, sources * CH // VIRTUAL_SOURCES, LANES), jnp.float32),
        pltpu.VMEM((2, sources, LAGS, CH), jnp.float32),
        pltpu.VMEM((sources if clears else 1, LAGS, CH), jnp.float32),
        pltpu.SemaphoreType.DMA((2, -(-sources // PART))),
        pltpu.SemaphoreType.DMA((TILE_CAP,)),
    ]
    if first:
        out_shape.append(jax.ShapeDtypeStruct((CHUNKS, LAGS, LANES), jnp.bfloat16))
        out_specs = out_specs + [held]
    results = pl.pallas_call(
        functools.partial(tile_kernel, config),
        out_shape=out_shape,
        in_specs=specs,
        out_specs=out_specs,
        scratch_shapes=scratch_shapes,
        input_output_aliases={} if first else {len(operands) - 1: 0},
        compiler_params=pltpu.CompilerParams(vmem_limit_bytes=VMEM_BYTES),
        cost_estimate=pl.CostEstimate(
            flops=COSTS[phase - 1] * sources * CH * LAGS * 2 * FREQS,
            bytes_accessed=1024 * 1024,
            transcendentals=0,
        ),
        name="tiles{}".format(phase),
    )(*operands)
    return results if first else results[0]


def after_kernel(count, *refs):
    for i in range(count):
        refs[count + 2 + i][...] = refs[1 + i][...]


def after(out, *blocks):
    held = pl.BlockSpec(memory_space=pltpu.VMEM)
    anywhere = pl.BlockSpec(memory_space=pl.ANY)
    arrays = (out, *blocks)
    return pl.pallas_call(
        functools.partial(after_kernel, len(blocks)),
        out_shape=[jax.ShapeDtypeStruct(a.shape, a.dtype) for a in arrays],
        in_specs=[anywhere] + [held] * len(blocks),
        out_specs=[anywhere] + [held] * len(blocks),
        input_output_aliases={0: 0},
        compiler_params=pltpu.CompilerParams(vmem_limit_bytes=VMEM_BYTES),
        name="after",
    )(*arrays)


def paired_kernel(mine, other, out):
    out[0], out[1] = mine[...], other[...]


def paired(mine, other):
    return pl.pallas_call(
        paired_kernel,
        out_shape=jax.ShapeDtypeStruct((2, *mine.shape), mine.dtype),
        in_specs=[pl.BlockSpec(memory_space=pltpu.VMEM)] * 2,
        out_specs=pl.BlockSpec(memory_space=pltpu.VMEM),
        compiler_params=pltpu.CompilerParams(vmem_limit_bytes=VMEM_BYTES),
        name="paired",
    )(mine, other)


def per_device(samples, pair_tiles):
    devices = lax.axis_size("chan")
    members = lax.axis_size("win")
    windows = samples.shape[0] * members
    sources = VIRTUAL_SOURCES // members
    scale = 1.0 / math.sqrt(FREQS * windows)

    def arriving(block, *routes):
        pairs = []
        for i in range(devices):
            for w in range(members):
                j = i + routes[w % len(routes)][i % 4]
                if 0 <= j < devices:
                    pairs.append((j * members + w, i * members + w))
        return lax.ppermute(block, ("chan", "win"), pairs)

    def swapped(block):
        return lax.ppermute(block, "win", [(0, 1), (1, 0)])

    def gathered(block):
        return lax.all_gather(block, "win", axis=0)

    flip_x, flip_y = (1, -1, 1, -1), (2, 2, -2, -2)
    to_third, to_fourth = (-2, 2, -2, 2), (-4, -4, 4, 4)

    pairs = pair_tiles.T
    own = whiten(samples)
    call = functools.partial(tile_call, sources=sources, windows=windows, scale=scale)
    if members == 2:
        blocks = [own, swapped(own)]
        near = arriving(paired(*blocks), flip_x, flip_y)
        layout = ((0, "own", 2),)
        out, inverse = call(1, [pairs], layout, blocks, out=None)
        known = [pairs, inverse]
        out, near = after(out, near)
        far = arriving(near, to_third, to_fourth)
        blocks = blocks + [near, swapped(near)]
        layout = layout + ((1, "two", 2),)
        out = call(2, known, layout, blocks, out=out, clears=True)
        out, far = after(out, far)
        far = [far, swapped(far)]
        out = call(3, known, layout + ((FAR, "two", 1),), blocks + far[:1], out=out)
        return call(4, known, layout + ((FAR, "two", 2),), blocks + far, out=out)
    layout = tuple((place, "all", 1) for place in range(NEARBY))
    near = [arriving(own, flip_x), arriving(own, flip_y)]
    blocks = [gathered(own)]
    out, inverse = call(1, [pairs], layout[:1], blocks, out=None)
    known = [pairs, inverse]
    far = [arriving(near[0], to_third), arriving(near[1], to_fourth)]
    blocks = blocks + [gathered(block) for block in near]
    out = call(2, known, layout[:FAR], blocks, out=out, clears=True)
    blocks = blocks + [gathered(block) for block in far]
    return call(3, known, layout, blocks, out=out)


def solution(mesh):
    placed = (P("win", "chan", None), P())
    return jax.shard_map(
        per_device,
        mesh=mesh,
        in_specs=placed,
        out_specs=P("chan", "win", None, None),
        check_vma=False,
    )
```
